256 devices in a mesh: pipe: 8 (over y, core), hidden: 32 (over z, x).
Axes of the slice: x: 4, y: 4, z: 8, core: 2. Of those that a mesh axis runs over, the one named last changes fastest.
Arguments:
- acts: bfloat16 [8, 1024, 16384], P('pipe', None, 'hidden'), may hold values from -6 to 6
- factors: bfloat16 [8, 4, 128, 128, 128], P('pipe', None, 'hidden'), may hold values from -0.5 to 0.5
- cotangent: bfloat16 [1024, 16384], P(None, 'hidden'), may hold values from -6 to 6
Outputs:
- input_grads: bfloat16 [8, 1024, 16384], P('pipe', None, 'hidden')
- factor_grads: float32 [8, 4, 128, 128, 128], P('pipe', None, 'hidden')
The draws below stay inside these ranges and needn't reach their ends.
All inputs are finite; a program needn't handle non-finite values.
Results may differ from the reference program's by a relative error of at most 0.03.
Values may be sent and summed in bfloat16 or wider, within the bound.
A program may use at most 64 MiB of HBM per device.

```python
import jax
import jax.numpy as jnp

BLK = 128
D = 16384
TOKENS = 1024
LAYERS = 8


def block_scale(key, shape, cuts, smallest, largest):
    gain, own = 1.0, jax.random.fold_in(key, 6)
    for dim, blocks in cuts:
        heights = jnp.exp(jax.random.uniform(jax.random.fold_in(own, dim), (blocks,), jnp.float32, smallest / len(cuts), largest / len(cuts)))
        gain = gain * jnp.repeat(heights, shape[dim] // blocks).reshape([-1 if axis == dim else 1 for axis in range(len(shape))])
    return gain


def scatter_about(stream_key, extent, deviation, reach, shards=(), kind=jnp.bfloat16):
    result = jax.random.normal(stream_key, extent, jnp.float32) * deviation
    if len(shards) > 0:
        result = block_scale(stream_key, extent, shards, -0.22, 0.18) * result
    return jnp.clip(result, min=-reach, max=reach).astype(kind)


def setup_inputs(seed: int = 0) -> dict:
    splits = jax.random.split(jax.random.key(seed), 4)
    return {
        "acts": scatter_about(splits[0], (LAYERS, TOKENS, D), 1.0, 6.0, ((0, 8), (2, 32))),
        "factors": scatter_about(splits[1], (LAYERS, 4, BLK, BLK, BLK), BLK ** -0.5, 0.5, ((0, 8), (2, 32))),
        "cotangent": scatter_about(splits[2], (TOKENS, D), 1.0, 6.0, ((1, 32),)),
    }


def gelu_slope(value):
    coeff = 0.7978845608028654
    inner = coeff * (value + 0.044715 * value ** 3)
    tangent = jnp.tanh(inner)
    return 0.5 * (1.0 + tangent) + 0.5 * value * (1.0 - tangent * tangent) * coeff * (1.0 + 3.0 * 0.044715 * value * value)

def monarch(inputs, right_factor, left_factor):
    block_grouped = inputs.reshape(TOKENS, BLK, BLK).astype(jnp.float32)
    mixed_output = jnp.einsum('nhl,hpl->nhp', block_grouped, right_factor.astype(jnp.float32)).astype(jnp.bfloat16)
    final_result = jnp.einsum('wbu,umb->wum', mixed_output.astype(jnp.float32), left_factor.astype(jnp.float32))
    return (final_result.reshape(TOKENS, D), mixed_output)

def monarch_grad(grad_out, mixed_output, inputs, right_factor, left_factor):
    block_gradient = grad_out.reshape(TOKENS, BLK, BLK).astype(jnp.float32)
    left_factor_gradient = jnp.einsum('mox,mzo->oxz', block_gradient, mixed_output.astype(jnp.float32))
    mixed_gradient = jnp.einsum('pxb,xbq->pqx', block_gradient, left_factor.astype(jnp.float32)).astype(jnp.bfloat16)
    block_inputs = inputs.reshape(TOKENS, BLK, BLK).astype(jnp.float32)
    right_factor_gradient = jnp.einsum('hxp,hxs->xps', mixed_gradient.astype(jnp.float32), block_inputs)
    input_gradient = jnp.einsum('joe,oex->jox', mixed_gradient.astype(jnp.float32), right_factor.astype(jnp.float32))
    return (input_gradient.reshape(TOKENS, D), right_factor_gradient, left_factor_gradient)

def layer_grad(inputs, weights, grad_out):
    hidden_pre, mixed_one = monarch(inputs, weights[0], weights[1])
    activ = jax.nn.gelu(hidden_pre, approximate=True).astype(jnp.bfloat16)
    unused, mixed_two = monarch(activ, weights[2], weights[3])
    grad_act, grad_r2, grad_l2 = monarch_grad(grad_out, mixed_two, activ, weights[2], weights[3])
    grad_hid = (grad_act * gelu_slope(hidden_pre)).astype(jnp.bfloat16)
    grad_x, grad_r1, grad_l1 = monarch_grad(grad_hid, mixed_one, inputs, weights[0], weights[1])
    input_gradient = (grad_out.astype(jnp.float32) + grad_x).astype(jnp.bfloat16)
    scale = TOKENS ** (-0.5)
    grads = jnp.stack([grad_r1, grad_l1, grad_r2, grad_l2]) * scale
    return (input_gradient, grads)

def reference(acts, factors, cotangent):
    carried = cotangent
    inputs_list = [None] * LAYERS
    grads_list = [None] * LAYERS
    for layer in range(LAYERS - 1, -1, -1):
        carried, grads = layer_grad(acts[layer], factors[layer], carried)
        inputs_list[layer] = carried
        grads_list[layer] = grads
    return (jnp.stack(inputs_list), jnp.stack(grads_list))
```

```python
import jax
import jax.numpy as jnp
from jax import lax
from jax.experimental import pallas as pl
from jax.experimental.pallas import tpu as pltpu
from jax.sharding import PartitionSpec as P

MESH = pl.DeviceIdType.MESH
BF = jnp.bfloat16
F32 = jnp.float32
N = 128
OWN = 4
FEAT = OWN * N
LAYERS = 8
PEERS = 32
PIECE = OWN * OWN
R1, L1, R2, L2 = 0, 1, 2, 3
U1, U2, D1, D2 = 0, 1, 2, 3
HALF = FEAT // 2


def dot(a, b, ca, cb):
    return lax.dot_general(a, b, (((ca,), (cb,)), ((), ())), preferred_element_type=F32)


def blk(i, size=N):
    return pl.ds(i * size, size)


def kernel(
    acts, factors, cot, gin, gfac,
    fac, wts, xs, gs, send, recv, st, vu1, vd2, vd1, vu2, act, slope, dh, pg, px, hs, home, fin,
    lsem, a_s, a_r, w_s, w_r, f_s, x_s, x_r, g_s, g_r, p_s, p_r, h_s, h_r,
):
    p = lax.axis_index("pipe")
    h = lax.axis_index("hidden")
    z, x = h // 4, lax.rem(h, 4)
    y, c = p // 2, lax.rem(p, 2)
    partner = p + 1 - 2 * c
    last = LAYERS - 1

    fac_in = pltpu.make_async_copy(factors, fac, lsem.at[0])
    cot_in = pltpu.make_async_copy(cot.at[pl.ds(pl.multiple_of(p * N, N), N)], gs.at[LAYERS], lsem.at[1])
    x_in = pltpu.make_async_copy(acts.at[pl.ds(pl.multiple_of(p * N, N), N)], xs.at[p], lsem.at[2])
    fac_in.start()
    cot_in.start()
    x_in.start()

    bar = pltpu.get_barrier_semaphore()

    def greet_hidden(k, _):
        pl.semaphore_signal(bar, inc=1, device_id={"hidden": lax.rem(h + k, PEERS)}, device_id_type=MESH)
        return 0

    def greet_pipe(k, _):
        pl.semaphore_signal(bar, inc=1, device_id={"pipe": lax.rem(p + k, LAYERS)}, device_id_type=MESH)
        return 0

    lax.fori_loop(1, PEERS, greet_hidden, 0)
    lax.fori_loop(1, LAYERS, greet_pipe, 0)

    fac_in.wait()

    def prepare(kind):
        if kind in (R1, R2):
            st[...] = fac[kind].astype(F32)
            for a in range(OWN):
                for cl in range(OWN):
                    rows = st[pl.ds(a * N + cl, N // OWN, stride=OWN), :]
                    wts[p, kind, pl.ds(a * N + cl * (N // OWN), N // OWN)] = rows.astype(BF)
        else:
            for b in range(OWN):
                wts[p, kind, blk(b)] = fac[kind, blk(b)].T

    for kind in (L2, R1, L1, R2):
        prepare(kind)
    pl.semaphore_wait(bar, PEERS - 1 + LAYERS - 1)

    def send_w(kind):
        for dest in (lax.rem(p + 2, LAYERS), lax.rem(p + 6, LAYERS), lax.rem(p + 4, LAYERS), partner):
            pltpu.make_async_remote_copy(
                src_ref=wts.at[p, kind], dst_ref=wts.at[p, kind], send_sem=w_s.at[kind], recv_sem=w_r.at[p, kind],
                device_id={"pipe": dest}, device_id_type=MESH,
            ).start()

    def send_x():
        def one(k, _):
            q = lax.rem(p + k, LAYERS)
            pltpu.make_async_remote_copy(
                src_ref=acts.at[pl.ds(pl.multiple_of(q * N, N), N)], dst_ref=xs.at[p], send_sem=x_s, recv_sem=x_r.at[p],
                device_id={"pipe": q}, device_id_type=MESH,
            ).start()
            return 0

        lax.fori_loop(1, LAYERS, one, 0)

    def fwd_copy(l, kind):
        return pltpu.make_async_remote_copy(
            src_ref=wts.at[l, kind], dst_ref=wts.at[l, kind], send_sem=f_s.at[l, kind], recv_sem=w_r.at[l, kind],
            device_id={"pipe": partner}, device_id_type=MESH,
        )

    def wait_w(l, kind):
        pltpu.make_async_copy(wts.at[l, kind], wts.at[l, kind], w_r.at[l, kind]).wait()

    def forward_w(l, kind):
        @pl.when(jnp.logical_and(lax.rem(l, 2) == c, l != p))
        def _():
            wait_w(l, kind)
            fwd_copy(l, kind).start()

    def need_w(l, kind):
        @pl.when(lax.rem(l, 2) != c)
        def _():
            wait_w(l, kind)

    def need_x(l):
        @pl.when(l == p)
        def _():
            x_in.wait()

        @pl.when(l != p)
        def _():
            pltpu.make_async_copy(xs.at[l], xs.at[l], x_r.at[l]).wait()

    def exchange(which, l):
        def one(k, _):
            i, j = k // 4, lax.rem(k, 4)
            hi, hj = (i + 1) // 2, (j + 1) // 2
            dz = 4 + hi * (1 - 2 * lax.rem(i, 2))
            dx = 2 + hj * (1 - 2 * lax.rem(j, 2))
            d = lax.rem(z + dz, 8) * 4 + lax.rem(x + dx, 4)
            pltpu.make_async_remote_copy(
                src_ref=send.at[which, l, pl.ds(pl.multiple_of(d * PIECE, PIECE), PIECE)],
                dst_ref=recv.at[which, l, pl.ds(pl.multiple_of(h * PIECE, PIECE), PIECE)],
                send_sem=a_s.at[which, l], recv_sem=a_r.at[which, l],
                device_id={"hidden": d}, device_id_type=MESH,
            ).start()
            return 0

        lax.fori_loop(0, PEERS - 1, one, 0)
        mine = pl.ds(pl.multiple_of(h * PIECE, PIECE), PIECE)
        recv[which, l, mine] = send[which, l, mine]

    def arrived(which, l):
        rows = recv.at[which, l, pl.ds(0, (PEERS - 1) * PIECE)]
        pltpu.make_async_copy(rows, rows, a_r.at[which, l]).wait()

    def produce_u(which, l, kind, value):
        for a in range(OWN):
            part = dot(wts[l, kind, blk(a)], value[:, a * N:(a + 1) * N], 1, 1)
            for cl in range(OWN):
                st[pl.ds(a * OWN + cl, PEERS, stride=PIECE), :] = part[cl * PEERS:(cl + 1) * PEERS]
        send[which, l] = st[...].astype(BF)
        exchange(which, l)

    def produce_d(which, l, kind, value):
        for b in range(OWN):
            st[pl.ds(b, N, stride=OWN), :] = dot(wts[l, kind, blk(b)], value[:, b * N:(b + 1) * N], 1, 1)
        send[which, l] = st[...].astype(BF)
        exchange(which, l)

    def take_u(which, l, out):
        arrived(which, l)
        st[...] = recv[which, l].astype(F32)
        for b in range(OWN):
            out[blk(b)] = st[pl.ds(b, N, stride=OWN), :].astype(BF)

    def take_d(which, l, out):
        arrived(which, l)
        st[...] = recv[which, l].astype(F32)
        for a in range(OWN):
            for cl in range(OWN):
                out[pl.ds(a * N + cl * PEERS, PEERS)] = st[pl.ds(a * OWN + cl, PEERS, stride=PIECE), :].astype(BF)

    def partial(l, kind, left, right):
        for b in range(OWN):
            pg[l, kind, blk(b)] = dot(left[blk(b)], right[:, blk(b)], 1, 0).astype(BF)

    def pair_copy(l, kind):
        return pltpu.make_async_remote_copy(
            src_ref=pg.at[l, kind, pl.ds(pl.multiple_of((1 - c) * HALF, HALF), HALF)], dst_ref=px.at[l, kind],
            send_sem=p_s.at[l, kind], recv_sem=p_r.at[l, kind], device_id={"pipe": partner}, device_id_type=MESH,
        )

    def home_copy(l, kind):
        return pltpu.make_async_remote_copy(
            src_ref=hs.at[l, kind], dst_ref=home.at[kind, p], send_sem=h_s.at[l, kind], recv_sem=h_r.at[kind],
            device_id={"pipe": l}, device_id_type=MESH,
        )

    def reduce(l, kind):
        pair_copy(l, kind).wait_recv()
        own = pg[l, kind, pl.ds(pl.multiple_of(c * HALF, HALF), HALF)]
        total = (own.astype(F32) + px[l, kind].astype(F32)).astype(BF)

        @pl.when(l == p)
        def _():
            home[kind, p] = total

        @pl.when(l != p)
        def _():
            hs[l, kind] = total
            home_copy(l, kind).start()

    def gin_copy(l):
        return pltpu.make_async_remote_copy(
            src_ref=gs.at[l], dst_ref=gin.at[pl.ds(pl.multiple_of(p * N, N), N)], send_sem=g_s.at[l], recv_sem=g_r,
            device_id={"pipe": l}, device_id_type=MESH,
        )

    def gin_own(l):
        return pltpu.make_async_copy(gs.at[l], gin.at[pl.ds(pl.multiple_of(p * N, N), N)], lsem.at[1])

    def first_half(l):
        need_w(l, R1)
        need_x(l)
        produce_u(U1, l, R1, xs[l])

    def second_half(l):
        slot = lax.rem(l, 2)
        need_w(l, L1)
        take_u(U1, l, vu1)
        coeff = 0.7978845608028654
        for b in range(OWN):
            v = dot(vu1[blk(b)], wts[l, L1, blk(b)], 0, 0)
            tangent = jnp.tanh(coeff * (v + 0.044715 * (v * v * v)))
            act[:, b * N:(b + 1) * N] = (0.5 * v * (1.0 + tangent)).astype(BF)
            slope[:, b * N:(b + 1) * N] = 0.5 * (1.0 + tangent) + 0.5 * v * (1.0 - tangent * tangent) * coeff * (
                1.0 + 3.0 * 0.044715 * v * v
            )
        need_w(l, R2)
        produce_u(U2, l, R2, act[...])

    @pl.when(p == last)
    def _():
        send_w(L2)
        send_w(R1)
        send_x()
        send_w(L1)
        send_w(R2)

    cot_in.wait()
    forward_w(last, L2)

    def step(s, _):
        l = last - s
        need_w(l, L2)
        produce_d(D2, l, L2, gs[l + 1])

        @pl.when(s == 0)
        def _():
            forward_w(last, R1)
            first_half(last)
            forward_w(last, L1)
            forward_w(last, R2)

        second_half(l)

        @pl.when(jnp.logical_and(s == 0, p == last - 1))
        def _():
            send_w(R1)
            send_x()
            send_w(L2)
            send_w(L1)
            send_w(R2)

        @pl.when(s > 0)
        def _():
            partial(l + 1, R1, vd1, xs.at[l + 1])
            pair_copy(l + 1, R1).start()
            reduce(l + 1, R2)
            reduce(l + 1, L1)
            reduce(l + 1, L2)

            @pl.when(s < last)
            def _():
                forward_w(l - 1, R1)
                forward_w(l - 1, L2)

        take_d(D2, l, vd2)
        for b in range(OWN):
            da = dot(vd2[blk(b)], wts[l, R2, blk(b)], 0, 0)
            dh[:, b * N:(b + 1) * N] = (da * slope[:, b * N:(b + 1) * N]).astype(BF)
        produce_d(D1, l, L1, dh[...])

        @pl.when(p == 5 - s)
        def _():
            send_w(R1)
            send_w(L2)
            send_x()
            send_w(L1)
            send_w(R2)

        partial(l, R2, vd2, act)
        pair_copy(l, R2).start()
        partial(l, L1, vu1, dh)
        pair_copy(l, L1).start()
        take_u(U2, l, vu2)
        partial(l, L2, vu2, gs.at[l + 1])
        pair_copy(l, L2).start()

        @pl.when(s > 0)
        def _():
            reduce(l + 1, R1)

        @pl.when(s < last)
        def _():
            @pl.when(s == 0)
            def _():
                forward_w(l - 1, R1)
                forward_w(l - 1, L2)

            first_half(l - 1)
            forward_w(l - 1, L1)
            forward_w(l - 1, R2)

        take_d(D1, l, vd1)
        for b in range(OWN):
            dx = dot(vd1[blk(b)], wts[l, R1, blk(b)], 0, 0)
            gs[l, :, b * N:(b + 1) * N] = (gs[l + 1, :, b * N:(b + 1) * N].astype(F32) + dx).astype(BF)

        @pl.when(l == p)
        def _():
            gin_own(l).start()

        @pl.when(l != p)
        def _():
            gin_copy(l).start()

        return 0

    lax.fori_loop(0, LAYERS, step, 0)

    partial(0, R1, vd1, xs.at[0])
    pair_copy(0, R1).start()
    reduce(0, R2)
    reduce(0, L1)
    reduce(0, L2)
    reduce(0, R1)

    def finish(kind):
        seven = home.at[kind, pl.ds(0, LAYERS - 1)]
        pltpu.make_async_copy(seven, seven, h_r.at[kind]).wait()
        for half in range(2):
            total = home[kind, half].astype(F32)
            for group in range(1, LAYERS // 2):
                total = total + home[kind, 2 * group + half].astype(F32)
            total = total * (LAYERS * N) ** -0.5
            for b in range(2):
                i = half * 2 + b
                own = total[b * N:(b + 1) * N]
                if kind in (R1, R2):
                    for cl in range(OWN):
                        fin[kind, pl.ds(i * N + cl, PEERS, stride=OWN), :] = own[cl * PEERS:(cl + 1) * PEERS]
                else:
                    fin[kind, blk(i)] = own.T
        out = pltpu.make_async_copy(fin.at[kind], gfac.at[kind], lsem.at[3 + kind])
        out.start()
        return out

    outs = [finish(kind) for kind in (R2, L1, L2, R1)]
    for out in outs:
        out.wait()

    seven = gin.at[pl.ds(0, (LAYERS - 1) * N)]
    pltpu.make_async_copy(seven, seven, g_r).wait()
    gin_own(p).wait()

    def drain(l, _):
        for which in range(4):
            rows = send.at[which, l, pl.ds(0, (PEERS - 1) * PIECE)]
            pltpu.make_async_copy(rows, rows, a_s.at[which, l]).wait()
        for kind in range(4):
            pair_copy(l, kind).wait_send()

            @pl.when(l != p)
            def _():
                home_copy(l, kind).wait_send()

            @pl.when(jnp.logical_and(lax.rem(l, 2) == c, l != p))
            def _():
                fwd_copy(l, kind).wait_send()

        @pl.when(l != p)
        def _():
            gin_copy(l).wait_send()

        return 0

    lax.fori_loop(0, LAYERS, drain, 0)
    for kind in range(4):
        four = wts.at[p, pl.ds(0, 4)]
        pltpu.make_async_copy(four, four, w_s.at[kind]).wait()
    pltpu.make_async_copy(seven, seven, x_s).wait()


def shards(acts, factors, cotangent):
    dma = pltpu.SemaphoreType.DMA
    gin, gfac = pl.pallas_call(
        kernel,
        name="monarch_backward",
        out_shape=(
            jax.ShapeDtypeStruct((LAYERS * N, FEAT), BF),
            jax.ShapeDtypeStruct((4, FEAT, N), F32),
        ),
        in_specs=[pl.BlockSpec(memory_space=pl.ANY)] * 3,
        out_specs=(pl.BlockSpec(memory_space=pl.ANY), pl.BlockSpec(memory_space=pl.ANY)),
        scratch_shapes=[
            pltpu.VMEM((4, FEAT, N), BF),
            pltpu.VMEM((LAYERS, 4, FEAT, N), BF),
            pltpu.VMEM((LAYERS, N, FEAT), BF),
            pltpu.VMEM((LAYERS + 1, N, FEAT), BF),
            pltpu.VMEM((4, LAYERS, FEAT, N), BF),
            pltpu.VMEM((4, LAYERS, FEAT, N), BF),
            pltpu.VMEM((FEAT, N), F32),
            pltpu.VMEM((FEAT, N), BF),
            pltpu.VMEM((FEAT, N), BF),
            pltpu.VMEM((FEAT, N), BF),
            pltpu.VMEM((FEAT, N), BF),
            pltpu.VMEM((N, FEAT), BF),
            pltpu.VMEM((N, FEAT), F32),
            pltpu.VMEM((N, FEAT), BF),
            pltpu.VMEM((LAYERS, 4, FEAT, N), BF),
            pltpu.VMEM((LAYERS, 4, HALF, N), BF),
            pltpu.VMEM((LAYERS, 4, HALF, N), BF),
            pltpu.VMEM((4, LAYERS, HALF, N), BF),
            pltpu.VMEM((4, FEAT, N), F32),
            dma((7,)),
            dma((4, LAYERS)), dma((4, LAYERS)),
            dma((4,)), dma((LAYERS, 4)), dma((LAYERS, 4)),
            dma, dma((LAYERS,)),
            dma((LAYERS,)), dma,
            dma((LAYERS, 4)), dma((LAYERS, 4)),
            dma((LAYERS, 4)), dma((4,)),
        ],
        compiler_params=pltpu.CompilerParams(
            collective_id=0, has_side_effects=True, vmem_limit_bytes=48 * 2**20
        ),
    )(acts.reshape(LAYERS * N, FEAT), factors.reshape(4, FEAT, N), cotangent)
    return gin.reshape(1, LAYERS * N, FEAT), gfac.reshape(1, 4, OWN, N, N)


def solution(mesh):
    in_specs = (P("pipe", None, "hidden"), P("pipe", None, "hidden", None, None), P(None, "hidden"))
    out_specs = (P("pipe", None, "hidden"), P("pipe", None, "hidden", None, None))
    return jax.shard_map(shards, mesh=mesh, in_specs=in_specs, out_specs=out_specs, check_vma=False)
```

```python
import jax
import jax.numpy as jnp
from jax import lax
from jax.experimental import pallas as pl
from jax.experimental.pallas import tpu as pltpu
from jax.sharding import PartitionSpec as P

MESH = pl.DeviceIdType.MESH
BF = jnp.bfloat16
F32 = jnp.float32
N = 128
OWN = 4
FEAT = OWN * N
LAYERS = 8
PEERS = 32
PIECE = OWN * OWN
R1, L1, R2, L2 = 0, 1, 2, 3
U1, U2, D1, D2 = 0, 1, 2, 3
HALF = FEAT // 2


def dot(a, b, ca, cb):
    return lax.dot_general(a, b, (((ca,), (cb,)), ((), ())), preferred_element_type=F32)


def blk(i, size=N):
    return pl.ds(i * size, size)


def kernel(
    acts, factors, cot, gin, gfac,
    fac, wts, xs, gs, send, recv, st, vu1, vd2, vd1, vu2, act, slope, dh, pg, px, hs, home, fin,
    lsem, a_s, a_r, w_s, w_r, f_s, x_s, x_r, g_s, g_r, p_s, p_r, h_s, h_r,
):
    p = lax.axis_index("pipe")
    h = lax.axis_index("hidden")
    z, x = h // 4, lax.rem(h, 4)
    y, c = p // 2, lax.rem(p, 2)
    partner = p + 1 - 2 * c
    last = LAYERS - 1

    fac_in = pltpu.make_async_copy(factors, fac, lsem.at[0])
    cot_in = pltpu.make_async_copy(cot.at[pl.ds(pl.multiple_of(p * N, N), N)], gs.at[LAYERS], lsem.at[1])
    x_in = pltpu.make_async_copy(acts.at[pl.ds(pl.multiple_of(p * N, N), N)], xs.at[p], lsem.at[2])
    fac_in.start()
    cot_in.start()
    x_in.start()

    bar = pltpu.get_barrier_semaphore()

    def greet_hidden(k, _):
        pl.semaphore_signal(bar, inc=1, device_id={"hidden": lax.rem(h + k, PEERS)}, device_id_type=MESH)
        return 0

    def greet_pipe(k, _):
        pl.semaphore_signal(bar, inc=1, device_id={"pipe": lax.rem(p + k, LAYERS)}, device_id_type=MESH)
        return 0

    lax.fori_loop(1, PEERS, greet_hidden, 0)
    lax.fori_loop(1, LAYERS, greet_pipe, 0)

    fac_in.wait()

    def prepare(kind):
        if kind in (R1, R2):
            st[...] = fac[kind].astype(F32)
            for a in range(OWN):
                for cl in range(OWN):
                    rows = st[pl.ds(a * N + cl, N // OWN, stride=OWN), :]
                    wts[p, kind, pl.ds(a * N + cl * (N // OWN), N // OWN)] = rows.astype(BF)
        else:
            for b in range(OWN):
                wts[p, kind, blk(b)] = fac[kind, blk(b)].T

    for kind in (L2, R1, L1, R2):
        prepare(kind)
    pl.semaphore_wait(bar, PEERS - 1 + LAYERS - 1)

    def send_w(kind):
        for dest in (lax.rem(p + 2, LAYERS), lax.rem(p + 6, LAYERS), lax.rem(p + 4, LAYERS), partner):
            pltpu.make_async_remote_copy(
                src_ref=wts.at[p, kind], dst_ref=wts.at[p, kind], send_sem=w_s.at[kind], recv_sem=w_r.at[p, kind],
                device_id={"pipe": dest}, device_id_type=MESH,
            ).start()

    def send_x():
        def one(k, _):
            q = lax.rem(p + k, LAYERS)
            pltpu.make_async_remote_copy(
                src_ref=acts.at[pl.ds(pl.multiple_of(q * N, N), N)], dst_ref=xs.at[p], send_sem=x_s, recv_sem=x_r.at[p],
                device_id={"pipe": q}, device_id_type=MESH,
            ).start()
            return 0

        lax.fori_loop(1, LAYERS, one, 0)

    def fwd_copy(l, kind):
        return pltpu.make_async_remote_copy(
            src_ref=wts.at[l, kind], dst_ref=wts.at[l, kind], send_sem=f_s.at[l, kind], recv_sem=w_r.at[l, kind],
            device_id={"pipe": partner}, device_id_type=MESH,
        )

    def wait_w(l, kind):
        pltpu.make_async_copy(wts.at[l, kind], wts.at[l, kind], w_r.at[l, kind]).wait()

    def forward_w(l, kind):
        @pl.when(jnp.logical_and(lax.rem(l, 2) == c, l != p))
        def _():
            wait_w(l, kind)
            fwd_copy(l, kind).start()

    def need_w(l, kind):
        @pl.when(lax.rem(l, 2) != c)
        def _():
            wait_w(l, kind)

    def need_x(l):
        @pl.when(l == p)
        def _():
            x_in.wait()

        @pl.when(l != p)
        def _():
            pltpu.make_async_copy(xs.at[l], xs.at[l], x_r.at[l]).wait()

    def exchange(which, l):
        def one(k, _):
            i, j = k // 4, lax.rem(k, 4)
            hi, hj = (i + 1) // 2, (j + 1) // 2
            dz = 4 + hi * (1 - 2 * lax.rem(i, 2))
            dx = 2 + hj * (1 - 2 * lax.rem(j, 2))
            d = lax.rem(z + dz, 8) * 4 + lax.rem(x + dx, 4)
            pltpu.make_async_remote_copy(
                src_ref=send.at[which, l, pl.ds(pl.multiple_of(d * PIECE, PIECE), PIECE)],
                dst_ref=recv.at[which, l, pl.ds(pl.multiple_of(h * PIECE, PIECE), PIECE)],
                send_sem=a_s.at[which, l], recv_sem=a_r.at[which, l],
                device_id={"hidden": d}, device_id_type=MESH,
            ).start()
            return 0

        lax.fori_loop(0, PEERS - 1, one, 0)
        mine = pl.ds(pl.multiple_of(h * PIECE, PIECE), PIECE)
        recv[which, l, mine] = send[which, l, mine]

    def arrived(which, l):
        rows = recv.at[which, l, pl.ds(0, (PEERS - 1) * PIECE)]
        pltpu.make_async_copy(rows, rows, a_r.at[which, l]).wait()

    def produce_u(which, l, kind, value):
        for a in range(OWN):
            part = dot(wts[l, kind, blk(a)], value[:, a * N:(a + 1) * N], 1, 1)
            for cl in range(OWN):
                st[pl.ds(a * OWN + cl, PEERS, stride=PIECE), :] = part[cl * PEERS:(cl + 1) * PEERS]
        send[which, l] = st[...].astype(BF)

    def produce_d(which, l, kind, value):
        for b in range(OWN):
            st[pl.ds(b, N, stride=OWN), :] = dot(wts[l, kind, blk(b)], value[:, b * N:(b + 1) * N], 1, 1)
        send[which, l] = st[...].astype(BF)
        exchange(which, l)

    def take_u(which, l, out):
        arrived(which, l)
        st[...] = recv[which, l].astype(F32)
        for b in range(OWN):
            out[blk(b)] = st[pl.ds(b, N, stride=OWN), :].astype(BF)

    def take_d(which, l, out):
        arrived(which, l)
        st[...] = recv[which, l].astype(F32)
        for a in range(OWN):
            for cl in range(OWN):
                out[pl.ds(a * N + cl * PEERS, PEERS)] = st[pl.ds(a * OWN + cl, PEERS, stride=PIECE), :].astype(BF)

    def partial(l, kind, left, right):
        for b in range(OWN):
            pg[l, kind, blk(b)] = dot(left[blk(b)], right[:, blk(b)], 1, 0).astype(BF)

    def pair_copy(l, kind):
        return pltpu.make_async_remote_copy(
            src_ref=pg.at[l, kind, pl.ds(pl.multiple_of((1 - c) * HALF, HALF), HALF)], dst_ref=px.at[l, kind],
            send_sem=p_s.at[l, kind], recv_sem=p_r.at[l, kind], device_id={"pipe": partner}, device_id_type=MESH,
        )

    def home_copy(l, kind):
        return pltpu.make_async_remote_copy(
            src_ref=hs.at[l, kind], dst_ref=home.at[kind, p], send_sem=h_s.at[l, kind], recv_sem=h_r.at[kind],
            device_id={"pipe": l}, device_id_type=MESH,
        )

    def reduce(l, kind):
        pair_copy(l, kind).wait_recv()
        own = pg[l, kind, pl.ds(pl.multiple_of(c * HALF, HALF), HALF)]
        total = (own.astype(F32) + px[l, kind].astype(F32)).astype(BF)

        @pl.when(l == p)
        def _():
            home[kind, p] = total

        @pl.when(l != p)
        def _():
            hs[l, kind] = total
            home_copy(l, kind).start()

    def gin_copy(l):
        return pltpu.make_async_remote_copy(
            src_ref=gs.at[l], dst_ref=gin.at[pl.ds(pl.multiple_of(p * N, N), N)], send_sem=g_s.at[l], recv_sem=g_r,
            device_id={"pipe": l}, device_id_type=MESH,
        )

    def gin_own(l):
        return pltpu.make_async_copy(gs.at[l], gin.at[pl.ds(pl.multiple_of(p * N, N), N)], lsem.at[1])

    def first_half(l):
        need_w(l, R1)
        need_x(l)
        produce_u(U1, l, R1, xs[l])

    def second_half(l):
        slot = lax.rem(l, 2)
        need_w(l, L1)
        take_u(U1, l, vu1.at[slot])
        coeff = 0.7978845608028654
        for b in range(OWN):
            v = dot(vu1[slot, blk(b)], wts[l, L1, blk(b)], 0, 0)
            tangent = jnp.tanh(coeff * (v + 0.044715 * (v * v * v)))
            act[slot, :, b * N:(b + 1) * N] = (0.5 * v * (1.0 + tangent)).astype(BF)
            slope[:, b * N:(b + 1) * N] = 0.5 * (1.0 + tangent) + 0.5 * v * (1.0 - tangent * tangent) * coeff * (
                1.0 + 3.0 * 0.044715 * v * v
            )
        need_w(l, R2)
        produce_u(U2, l, R2, act[slot])

    def send_all():
        send_w(L2)
        send_w(R1)
        send_x()
        send_w(L1)
        send_w(R2)

    @pl.when(p == last)
    def _():
        send_all()

    cot_in.wait()
    forward_w(last, L2)

    def step(s, _):
        l = last - s
        slot = lax.rem(l, 2)
        need_w(l, L2)
        produce_d(D2, l, L2, gs[l + 1])

        @pl.when(jnp.logical_and(s >= 2, l >= 1))
        def _():
            exchange(U1, l - 1)

        @pl.when(l == 0)
        def _():
            exchange(U2, l)

        @pl.when(s == 0)
        def _():
            pl.when(p == 5)(send_all)
            forward_w(l, R1)
            first_half(l)
            exchange(U1, l)
            pl.when(jnp.logical_or(p == 6, p < 5))(send_all)
            forward_w(l, L1)
            forward_w(l, R2)

        @pl.when(s <= 1)
        def _():
            second_half(l)

        @pl.when(s == 1)
        def _():
            forward_w(l - 1, R1)
            first_half(l - 1)
            exchange(U1, l - 1)

        @pl.when(s >= 1)
        def _():
            partial(l + 1, R1, vd1, xs.at[l + 1])
            pair_copy(l + 1, R1).start()
            take_u(U2, l + 1, vu2)
            partial(l + 1, L2, vu2, gs.at[l + 2])
            pair_copy(l + 1, L2).start()

            @pl.when(l >= 2)
            def _():
                forward_w(l - 2, R1)

            @pl.when(l >= 1)
            def _():
                forward_w(l - 1, L1)
                forward_w(l - 1, R2)
                forward_w(l - 1, L2)

        take_d(D2, l, vd2)
        for b in range(OWN):
            da = dot(vd2[blk(b)], wts[l, R2, blk(b)], 0, 0)
            dh[:, b * N:(b + 1) * N] = (da * slope[:, b * N:(b + 1) * N]).astype(BF)
        produce_d(D1, l, L1, dh[...])

        @pl.when(l >= 1)
        def _():
            exchange(U2, l)

        @pl.when(s == 0)
        def _():
            forward_w(l - 1, R1)
            first_half(l - 1)
            exchange(U1, l - 1)

        partial(l, R2, vd2, act.at[slot])
        pair_copy(l, R2).start()
        partial(l, L1, vu1.at[slot], dh)
        pair_copy(l, L1).start()

        @pl.when(jnp.logical_and(s >= 1, l >= 1))
        def _():
            second_half(l - 1)

        @pl.when(jnp.logical_and(s >= 1, l >= 2))
        def _():
            first_half(l - 2)

        @pl.when(s == 0)
        def _():
            forward_w(l - 1, L1)
            forward_w(l - 1, R2)
            forward_w(l - 1, L2)

        @pl.when(s >= 1)
        def _():
            reduce(l + 1, R1)
            reduce(l + 1, L2)

        @pl.when(l == 0)
        def _():
            take_u(U2, l, vu2)
            partial(l, L2, vu2, gs.at[l + 1])
            pair_copy(l, L2).start()

        reduce(l, R2)
        reduce(l, L1)

        @pl.when(l == 0)
        def _():
            reduce(l, L2)

        take_d(D1, l, vd1)
        for b in range(OWN):
            dx = dot(vd1[blk(b)], wts[l, R1, blk(b)], 0, 0)
            gs[l, :, b * N:(b + 1) * N] = (gs[l + 1, :, b * N:(b + 1) * N].astype(F32) + dx).astype(BF)

        @pl.when(l == p)
        def _():
            gin_own(l).start()

        @pl.when(l != p)
        def _():
            gin_copy(l).start()

        return 0

    lax.fori_loop(0, LAYERS, step, 0)

    partial(0, R1, vd1, xs.at[0])
    pair_copy(0, R1).start()
    reduce(0, R1)

    def finish(kind):
        seven = home.at[kind, pl.ds(0, LAYERS - 1)]
        pltpu.make_async_copy(seven, seven, h_r.at[kind]).wait()
        for half in range(2):
            total = home[kind, half].astype(F32)
            for group in range(1, LAYERS // 2):
                total = total + home[kind, 2 * group + half].astype(F32)
            total = total * (LAYERS * N) ** -0.5
            for b in range(2):
                i = half * 2 + b
                own = total[b * N:(b + 1) * N]
                if kind in (R1, R2):
                    for cl in range(OWN):
                        fin[kind, pl.ds(i * N + cl, PEERS, stride=OWN), :] = own[cl * PEERS:(cl + 1) * PEERS]
                else:
                    fin[kind, blk(i)] = own.T
        out = pltpu.make_async_copy(fin.at[kind], gfac.at[kind], lsem.at[3 + kind])
        out.start()
        return out

    outs = [finish(kind) for kind in (R2, L1, L2, R1)]
    for out in outs:
        out.wait()

    seven = gin.at[pl.ds(0, (LAYERS - 1) * N)]
    pltpu.make_async_copy(seven, seven, g_r).wait()
    gin_own(p).wait()

    def drain(l, _):
        for which in range(4):
            rows = send.at[which, l, pl.ds(0, (PEERS - 1) * PIECE)]
            pltpu.make_async_copy(rows, rows, a_s.at[which, l]).wait()
        for kind in range(4):
            pair_copy(l, kind).wait_send()

            @pl.when(l != p)
            def _():
                home_copy(l, kind).wait_send()

            @pl.when(jnp.logical_and(lax.rem(l, 2) == c, l != p))
            def _():
                fwd_copy(l, kind).wait_send()

        @pl.when(l != p)
        def _():
            gin_copy(l).wait_send()

        return 0

    lax.fori_loop(0, LAYERS, drain, 0)
    for kind in range(4):
        four = wts.at[p, pl.ds(0, 4)]
        pltpu.make_async_copy(four, four, w_s.at[kind]).wait()
    pltpu.make_async_copy(seven, seven, x_s).wait()


def shards(acts, factors, cotangent):
    dma = pltpu.SemaphoreType.DMA
    gin, gfac = pl.pallas_call(
        kernel,
        name="monarch_backward",
        out_shape=(
            jax.ShapeDtypeStruct((LAYERS * N, FEAT), BF),
            jax.ShapeDtypeStruct((4, FEAT, N), F32),
        ),
        in_specs=[pl.BlockSpec(memory_space=pl.ANY)] * 3,
        out_specs=(pl.BlockSpec(memory_space=pl.ANY), pl.BlockSpec(memory_space=pl.ANY)),
        scratch_shapes=[
            pltpu.VMEM((4, FEAT, N), BF),
            pltpu.VMEM((LAYERS, 4, FEAT, N), BF),
            pltpu.VMEM((LAYERS, N, FEAT), BF),
            pltpu.VMEM((LAYERS + 1, N, FEAT), BF),
            pltpu.VMEM((4, LAYERS, FEAT, N), BF),
            pltpu.VMEM((4, LAYERS, FEAT, N), BF),
            pltpu.VMEM((FEAT, N), F32),
            pltpu.VMEM((2, FEAT, N), BF),
            pltpu.VMEM((FEAT, N), BF),
            pltpu.VMEM((FEAT, N), BF),
            pltpu.VMEM((FEAT, N), BF),
            pltpu.VMEM((2, N, FEAT), BF),
            pltpu.VMEM((N, FEAT), F32),
            pltpu.VMEM((N, FEAT), BF),
            pltpu.VMEM((LAYERS, 4, FEAT, N), BF),
            pltpu.VMEM((LAYERS, 4, HALF, N), BF),
            pltpu.VMEM((LAYERS, 4, HALF, N), BF),
            pltpu.VMEM((4, LAYERS, HALF, N), BF),
            pltpu.VMEM((4, FEAT, N), F32),
            dma((7,)),
            dma((4, LAYERS)), dma((4, LAYERS)),
            dma((4,)), dma((LAYERS, 4)), dma((LAYERS, 4)),
            dma, dma((LAYERS,)),
            dma((LAYERS,)), dma,
            dma((LAYERS, 4)), dma((LAYERS, 4)),
            dma((LAYERS, 4)), dma((4,)),
        ],
        compiler_params=pltpu.CompilerParams(
            collective_id=0, has_side_effects=True, vmem_limit_bytes=63 * 2**20
        ),
    )(acts.reshape(LAYERS * N, FEAT), factors.reshape(4, FEAT, N), cotangent)
    return gin.reshape(1, LAYERS * N, FEAT), gfac.reshape(1, 4, OWN, N, N)


def solution(mesh):
    in_specs = (P("pipe", None, "hidden"), P("pipe", None, "hidden", None, None), P(None, "hidden"))
    out_specs = (P("pipe", None, "hidden"), P("pipe", None, "hidden", None, None))
    return jax.shard_map(shards, mesh=mesh, in_specs=in_specs, out_specs=out_specs, check_vma=False)
```

```python
import jax
import jax.numpy as jnp
from jax import lax
from jax.experimental import pallas as pl
from jax.experimental.pallas import tpu as pltpu
from jax.sharding import PartitionSpec as P

MESH = pl.DeviceIdType.MESH
BF = jnp.bfloat16
F32 = jnp.float32
N = 128
OWN = 4
FEAT = OWN * N
LAYERS = 8
PEERS = 32
PIECE = OWN * OWN
R1, L1, R2, L2 = 0, 1, 2, 3
U1, U2, D1, D2 = 0, 1, 2, 3
HALF = FEAT // 2
EARLY = 6
RELAYED = (R1, L1, R2,)


def dot(a, b, ca, cb):
    return lax.dot_general(a, b, (((ca,), (cb,)), ((), ())), preferred_element_type=F32)


def blk(i, size=N):
    return pl.ds(i * size, size)


def kernel(
    acts, factors, cot, gin, gfac,
    fac, wts, xs, gs, send, recv, st, vu1, vd2, vd1, vu2, act, slope, dh, pg, px, hs, home, fin,
    lsem, a_s, a_r, w_s, w_r, f_s, y_s, x_s, x_r, g_s, g_r, p_s, p_r, h_s, h_r,
):
    p = lax.axis_index("pipe")
    h = lax.axis_index("hidden")
    z, x = h // 4, lax.rem(h, 4)
    y, c = p // 2, lax.rem(p, 2)
    partner = p + 1 - 2 * c
    last = LAYERS - 1

    fac_in = pltpu.make_async_copy(factors, fac, lsem.at[0])
    cot_in = pltpu.make_async_copy(cot.at[pl.ds(pl.multiple_of(p * N, N), N)], gs.at[LAYERS], lsem.at[1])
    x_in = pltpu.make_async_copy(acts.at[pl.ds(pl.multiple_of(p * N, N), N)], xs.at[p], lsem.at[2])
    fac_in.start()
    cot_in.start()
    x_in.start()

    bar = pltpu.get_barrier_semaphore()

    def greet_hidden(k, _):
        pl.semaphore_signal(bar, inc=1, device_id={"hidden": lax.rem(h + k, PEERS)}, device_id_type=MESH)
        return 0

    def greet_pipe(k, _):
        pl.semaphore_signal(bar, inc=1, device_id={"pipe": lax.rem(p + k, LAYERS)}, device_id_type=MESH)
        return 0

    lax.fori_loop(1, PEERS, greet_hidden, 0)
    lax.fori_loop(1, LAYERS, greet_pipe, 0)

    fac_in.wait()

    def prepare(kind):
        if kind in (R1, R2):
            st[...] = fac[kind].astype(F32)
            for a in range(OWN):
                for cl in range(OWN):
                    rows = st[pl.ds(a * N + cl, N // OWN, stride=OWN), :]
                    wts[p, kind, pl.ds(a * N + cl * (N // OWN), N // OWN)] = rows.astype(BF)
        else:
            for b in range(OWN):
                wts[p, kind, blk(b)] = fac[kind, blk(b)].T

    for kind in (L2, R1, L1, R2):
        prepare(kind)
    pl.semaphore_wait(bar, PEERS - 1 + LAYERS - 1)

    def send_w(kind):
        def to(dest):
            pltpu.make_async_remote_copy(
                src_ref=wts.at[p, kind], dst_ref=wts.at[p, kind], send_sem=w_s.at[kind], recv_sem=w_r.at[p, kind],
                device_id={"pipe": dest}, device_id_type=MESH,
            ).start()

        to(lax.rem(p + 2, LAYERS))
        to(lax.rem(p + 6, LAYERS))
        if kind in RELAYED:
            pl.when(p < EARLY)(lambda: to(lax.rem(p + 4, LAYERS)))
        else:
            to(lax.rem(p + 4, LAYERS))
        to(partner)

    def send_x():
        def one(k, _):
            q = lax.rem(p + k, LAYERS)
            pltpu.make_async_remote_copy(
                src_ref=acts.at[pl.ds(pl.multiple_of(q * N, N), N)], dst_ref=xs.at[p], send_sem=x_s, recv_sem=x_r.at[p],
                device_id={"pipe": q}, device_id_type=MESH,
            ).start()
            return 0

        lax.fori_loop(1, LAYERS, one, 0)

    def fwd_copy(l, kind):
        return pltpu.make_async_remote_copy(
            src_ref=wts.at[l, kind], dst_ref=wts.at[l, kind], send_sem=f_s.at[l, kind], recv_sem=w_r.at[l, kind],
            device_id={"pipe": partner}, device_id_type=MESH,
        )

    def relay_copy(l, kind):
        return pltpu.make_async_remote_copy(
            src_ref=wts.at[l, kind], dst_ref=wts.at[l, kind], send_sem=y_s.at[l, kind], recv_sem=w_r.at[l, kind],
            device_id={"pipe": lax.rem(l + 4, LAYERS)}, device_id_type=MESH,
        )

    def relays(l):
        return jnp.logical_and(l >= EARLY, p == lax.rem(l + 6, LAYERS))

    def wait_w(l, kind):
        pltpu.make_async_copy(wts.at[l, kind], wts.at[l, kind], w_r.at[l, kind]).wait()

    def forward_w(l, kind):
        @pl.when(jnp.logical_and(lax.rem(l, 2) == c, l != p))
        def _():
            wait_w(l, kind)
            if kind in RELAYED:
                pl.when(relays(l))(lambda: relay_copy(l, kind).start())
            fwd_copy(l, kind).start()

    def need_w(l, kind):
        @pl.when(lax.rem(l, 2) != c)
        def _():
            wait_w(l, kind)

    def need_x(l):
        @pl.when(l == p)
        def _():
            x_in.wait()

        @pl.when(l != p)
        def _():
            pltpu.make_async_copy(xs.at[l], xs.at[l], x_r.at[l]).wait()

    def exchange(which, l):
        def one(k, _):
            i, j = k // 4, lax.rem(k, 4)
            hi, hj = (i + 1) // 2, (j + 1) // 2
            dz = 4 + hi * (1 - 2 * lax.rem(i, 2))
            dx = 2 + hj * (1 - 2 * lax.rem(j, 2))
            d = lax.rem(z + dz, 8) * 4 + lax.rem(x + dx, 4)
            pltpu.make_async_remote_copy(
                src_ref=send.at[which, l, pl.ds(pl.multiple_of(d * PIECE, PIECE), PIECE)],
                dst_ref=recv.at[which, l, pl.ds(pl.multiple_of(h * PIECE, PIECE), PIECE)],
                send_sem=a_s.at[which, l], recv_sem=a_r.at[which, l],
                device_id={"hidden": d}, device_id_type=MESH,
            ).start()
            return 0

        lax.fori_loop(0, PEERS - 1, one, 0)
        mine = pl.ds(pl.multiple_of(h * PIECE, PIECE), PIECE)
        recv[which, l, mine] = send[which, l, mine]

    def arrived(which, l):
        rows = recv.at[which, l, pl.ds(0, (PEERS - 1) * PIECE)]
        pltpu.make_async_copy(rows, rows, a_r.at[which, l]).wait()

    def produce_u(which, l, kind, value):
        for a in range(OWN):
            part = dot(wts[l, kind, blk(a)], value[:, a * N:(a + 1) * N], 1, 1)
            for cl in range(OWN):
                st[pl.ds(a * OWN + cl, PEERS, stride=PIECE), :] = part[cl * PEERS:(cl + 1) * PEERS]
        send[which, l] = st[...].astype(BF)

    def produce_d(which, l, kind, value):
        for b in range(OWN):
            st[pl.ds(b, N, stride=OWN), :] = dot(wts[l, kind, blk(b)], value[:, b * N:(b + 1) * N], 1, 1)
        send[which, l] = st[...].astype(BF)
        exchange(which, l)

    def take_u(which, l, out):
        arrived(which, l)
        st[...] = recv[which, l].astype(F32)
        for b in range(OWN):
            out[blk(b)] = st[pl.ds(b, N, stride=OWN), :].astype(BF)

    def take_d(which, l, out):
        arrived(which, l)
        st[...] = recv[which, l].astype(F32)
        for a in range(OWN):
            for cl in range(OWN):
                out[pl.ds(a * N + cl * PEERS, PEERS)] = st[pl.ds(a * OWN + cl, PEERS, stride=PIECE), :].astype(BF)

    def partial(l, kind, left, right):
        for b in range(OWN):
            pg[l, kind, blk(b)] = dot(left[blk(b)], right[:, blk(b)], 1, 0).astype(BF)

    def pair_copy(l, kind):
        return pltpu.make_async_remote_copy(
            src_ref=pg.at[l, kind, pl.ds(pl.multiple_of((1 - c) * HALF, HALF), HALF)], dst_ref=px.at[l, kind],
            send_sem=p_s.at[l, kind], recv_sem=p_r.at[l, kind], device_id={"pipe": partner}, device_id_type=MESH,
        )

    def home_copy(l, kind):
        return pltpu.make_async_remote_copy(
            src_ref=hs.at[l, kind], dst_ref=home.at[kind, p], send_sem=h_s.at[l, kind], recv_sem=h_r.at[kind],
            device_id={"pipe": l}, device_id_type=MESH,
        )

    def reduce(l, kind):
        pair_copy(l, kind).wait_recv()
        own = pg[l, kind, pl.ds(pl.multiple_of(c * HALF, HALF), HALF)]
        total = (own.astype(F32) + px[l, kind].astype(F32)).astype(BF)

        @pl.when(l == p)
        def _():
            home[kind, p] = total

        @pl.when(l != p)
        def _():
            hs[l, kind] = total
            home_copy(l, kind).start()

    def gin_copy(l):
        return pltpu.make_async_remote_copy(
            src_ref=gs.at[l], dst_ref=gin.at[pl.ds(pl.multiple_of(p * N, N), N)], send_sem=g_s.at[l], recv_sem=g_r,
            device_id={"pipe": l}, device_id_type=MESH,
        )

    def gin_own(l):
        return pltpu.make_async_copy(gs.at[l], gin.at[pl.ds(pl.multiple_of(p * N, N), N)], lsem.at[1])

    def first_half(l):
        need_w(l, R1)
        need_x(l)
        produce_u(U1, l, R1, xs[l])

    def second_half(l):
        slot = lax.rem(l, 2)
        need_w(l, L1)
        take_u(U1, l, vu1.at[slot])
        coeff = 0.7978845608028654
        for b in range(OWN):
            v = dot(vu1[slot, blk(b)], wts[l, L1, blk(b)], 0, 0)
            tangent = jnp.tanh(coeff * (v + 0.044715 * (v * v * v)))
            act[slot, :, b * N:(b + 1) * N] = (0.5 * v * (1.0 + tangent)).astype(BF)
            slope[:, b * N:(b + 1) * N] = 0.5 * (1.0 + tangent) + 0.5 * v * (1.0 - tangent * tangent) * coeff * (
                1.0 + 3.0 * 0.044715 * v * v
            )
        need_w(l, R2)
        produce_u(U2, l, R2, act[slot])

    def send_all():
        send_w(L2)
        send_w(R1)
        send_x()
        send_w(L1)
        send_w(R2)

    @pl.when(p == last)
    def _():
        send_all()

    cot_in.wait()
    forward_w(last, L2)

    def step(s, _):
        l = last - s
        slot = lax.rem(l, 2)
        need_w(l, L2)
        produce_d(D2, l, L2, gs[l + 1])

        @pl.when(jnp.logical_and(s >= 2, l >= 1))
        def _():
            exchange(U1, l - 1)

        @pl.when(s == 0)
        def _():
            pl.when(p == 5)(send_all)
            forward_w(l, R1)
            first_half(l)
            exchange(U1, l)
            pl.when(jnp.logical_or(p == 6, p < 5))(send_all)
            forward_w(l, L1)
            forward_w(l, R2)

        @pl.when(s <= 1)
        def _():
            second_half(l)

        @pl.when(s == 1)
        def _():
            forward_w(l - 1, R1)
            first_half(l - 1)
            exchange(U1, l - 1)

        @pl.when(s >= 1)
        def _():
            partial(l + 1, R1, vd1, xs.at[l + 1])
            pair_copy(l + 1, R1).start()
            take_u(U2, l + 1, vu2)
            partial(l + 1, L2, vu2, gs.at[l + 2])
            pair_copy(l + 1, L2).start()

            @pl.when(l >= 2)
            def _():
                forward_w(l - 2, R1)

            @pl.when(l >= 1)
            def _():
                forward_w(l - 1, L1)
                forward_w(l - 1, R2)
                forward_w(l - 1, L2)

        @pl.when(l == 0)
        def _():
            take_u(U2, l, vu2)
            partial(l, L2, vu2, gs.at[l + 1])
            pair_copy(l, L2).start()

        take_d(D2, l, vd2)
        for b in range(OWN):
            da = dot(vd2[blk(b)], wts[l, R2, blk(b)], 0, 0)
            dh[:, b * N:(b + 1) * N] = (da * slope[:, b * N:(b + 1) * N]).astype(BF)
        produce_d(D1, l, L1, dh[...])

        @pl.when(l >= 1)
        def _():
            exchange(U2, l)

        @pl.when(s == 0)
        def _():
            forward_w(l - 1, R1)
            first_half(l - 1)
            exchange(U1, l - 1)

        partial(l, R2, vd2, act.at[slot])
        pair_copy(l, R2).start()
        partial(l, L1, vu1.at[slot], dh)
        pair_copy(l, L1).start()

        @pl.when(jnp.logical_and(s >= 1, l >= 1))
        def _():
            second_half(l - 1)

        @pl.when(jnp.logical_and(s >= 1, l >= 2))
        def _():
            first_half(l - 2)

        @pl.when(l == 1)
        def _():
            exchange(U2, l - 1)

        @pl.when(s == 0)
        def _():
            forward_w(l - 1, L1)
            forward_w(l - 1, R2)
            forward_w(l - 1, L2)

        @pl.when(s >= 1)
        def _():
            reduce(l + 1, R1)
            reduce(l + 1, L2)

        pl.when(l == 0)(lambda: reduce(l, L2))

        reduce(l, R2)
        reduce(l, L1)

        take_d(D1, l, vd1)

        @pl.when(l == 0)
        def _():
            partial(l, R1, vd1, xs.at[l])
            pair_copy(l, R1).start()

        for b in range(OWN):
            dx = dot(vd1[blk(b)], wts[l, R1, blk(b)], 0, 0)
            gs[l, :, b * N:(b + 1) * N] = (gs[l + 1, :, b * N:(b + 1) * N].astype(F32) + dx).astype(BF)

        @pl.when(l == p)
        def _():
            gin_own(l).start()

        @pl.when(l != p)
        def _():
            gin_copy(l).start()

        return 0

    lax.fori_loop(0, LAYERS, step, 0)

    reduce(0, R1)

    def finish(kind):
        seven = home.at[kind, pl.ds(0, LAYERS - 1)]
        pltpu.make_async_copy(seven, seven, h_r.at[kind]).wait()
        for half in range(2):
            total = home[kind, half].astype(F32)
            for group in range(1, LAYERS // 2):
                total = total + home[kind, 2 * group + half].astype(F32)
            total = total * (LAYERS * N) ** -0.5
            for b in range(2):
                i = half * 2 + b
                own = total[b * N:(b + 1) * N]
                if kind in (R1, R2):
                    for cl in range(OWN):
                        fin[kind, pl.ds(i * N + cl, PEERS, stride=OWN), :] = own[cl * PEERS:(cl + 1) * PEERS]
                else:
                    fin[kind, blk(i)] = own.T
        out = pltpu.make_async_copy(fin.at[kind], gfac.at[kind], lsem.at[3 + kind])
        out.start()
        return out

    outs = [finish(kind) for kind in (R2, L1, L2, R1)]
    for out in outs:
        out.wait()

    seven = gin.at[pl.ds(0, (LAYERS - 1) * N)]
    pltpu.make_async_copy(seven, seven, g_r).wait()
    gin_own(p).wait()

    def drain(l, _):
        for which in range(4):
            rows = send.at[which, l, pl.ds(0, (PEERS - 1) * PIECE)]
            pltpu.make_async_copy(rows, rows, a_s.at[which, l]).wait()
        for kind in range(4):
            pair_copy(l, kind).wait_send()

            @pl.when(l != p)
            def _():
                home_copy(l, kind).wait_send()

            @pl.when(jnp.logical_and(lax.rem(l, 2) == c, l != p))
            def _():
                fwd_copy(l, kind).wait_send()
                if kind in RELAYED:
                    pl.when(relays(l))(lambda: relay_copy(l, kind).wait_send())

        @pl.when(l != p)
        def _():
            gin_copy(l).wait_send()

        return 0

    lax.fori_loop(0, LAYERS, drain, 0)
    def sent(kind, copies):
        part = wts.at[p, pl.ds(0, copies)]
        pltpu.make_async_copy(part, part, w_s.at[kind]).wait()

    for kind in range(4):
        if kind in RELAYED:
            pl.when(p < EARLY)(lambda: sent(kind, 4))
            pl.when(p >= EARLY)(lambda: sent(kind, 3))
        else:
            sent(kind, 4)
    pltpu.make_async_copy(seven, seven, x_s).wait()


def shards(acts, factors, cotangent):
    dma = pltpu.SemaphoreType.DMA
    gin, gfac = pl.pallas_call(
        kernel,
        name="monarch_backward",
        out_shape=(
            jax.ShapeDtypeStruct((LAYERS * N, FEAT), BF),
            jax.ShapeDtypeStruct((4, FEAT, N), F32),
        ),
        in_specs=[pl.BlockSpec(memory_space=pl.ANY)] * 3,
        out_specs=(pl.BlockSpec(memory_space=pl.ANY), pl.BlockSpec(memory_space=pl.ANY)),
        scratch_shapes=[
            pltpu.VMEM((4, FEAT, N), BF),
            pltpu.VMEM((LAYERS, 4, FEAT, N), BF),
            pltpu.VMEM((LAYERS, N, FEAT), BF),
            pltpu.VMEM((LAYERS + 1, N, FEAT), BF),
            pltpu.VMEM((4, LAYERS, FEAT, N), BF),
            pltpu.VMEM((4, LAYERS, FEAT, N), BF),
            pltpu.VMEM((FEAT, N), F32),
            pltpu.VMEM((2, FEAT, N), BF),
            pltpu.VMEM((FEAT, N), BF),
            pltpu.VMEM((FEAT, N), BF),
            pltpu.VMEM((FEAT, N), BF),
            pltpu.VMEM((2, N, FEAT), BF),
            pltpu.VMEM((N, FEAT), F32),
            pltpu.VMEM((N, FEAT), BF),
            pltpu.VMEM((LAYERS, 4, FEAT, N), BF),
            pltpu.VMEM((LAYERS, 4, HALF, N), BF),
            pltpu.VMEM((LAYERS, 4, HALF, N), BF),
            pltpu.VMEM((4, LAYERS, HALF, N), BF),
            pltpu.VMEM((4, FEAT, N), F32),
            dma((7,)),
            dma((4, LAYERS)), dma((4, LAYERS)),
            dma((4,)), dma((LAYERS, 4)), dma((LAYERS, 4)), dma((LAYERS, 4)),
            dma, dma((LAYERS,)),
            dma((LAYERS,)), dma,
            dma((LAYERS, 4)), dma((LAYERS, 4)),
            dma((LAYERS, 4)), dma((4,)),
        ],
        compiler_params=pltpu.CompilerParams(
            collective_id=0, has_side_effects=True, vmem_limit_bytes=63 * 2**20
        ),
    )(acts.reshape(LAYERS * N, FEAT), factors.reshape(4, FEAT, N), cotangent)
    return gin.reshape(1, LAYERS * N, FEAT), gfac.reshape(1, 4, OWN, N, N)


def solution(mesh):
    in_specs = (P("pipe", None, "hidden"), P("pipe", None, "hidden", None, None), P(None, "hidden"))
    out_specs = (P("pipe", None, "hidden"), P("pipe", None, "hidden", None, None))
    return jax.shard_map(shards, mesh=mesh, in_specs=in_specs, out_specs=out_specs, check_vma=False)
```

```python
import jax
import jax.numpy as jnp
from jax import lax
from jax.experimental import pallas as pl
from jax.experimental.pallas import tpu as pltpu
from jax.sharding import PartitionSpec as P

MESH = pl.DeviceIdType.MESH
BF = jnp.bfloat16
F32 = jnp.float32
N = 128
OWN = 4
FEAT = OWN * N
LAYERS = 8
PEERS = 32
PIECE = OWN * OWN
R1, L1, R2, L2 = 0, 1, 2, 3
U1, U2, D1, D2 = 0, 1, 2, 3
HALF = FEAT // 2
EARLY = 6
RELAYED = (R1, L1, R2,)


def dot(a, b, ca, cb):
    return lax.dot_general(a, b, (((ca,), (cb,)), ((), ())), preferred_element_type=F32)


def blk(i, size=N):
    return pl.ds(i * size, size)


def kernel(
    acts, factors, cot, gin, gfac,
    fac, wts, xs, gs, send, recv, st, vu1, vd2, vd1, vu2, act, slope, dh, pg, px, hs, home, fin,
    lsem, a_s, a_r, w_s, w_r, f_s, y_s, x_s, x_r, g_s, g_r, p_s, p_r, h_s, h_r,
):
    p = lax.axis_index("pipe")
    h = lax.axis_index("hidden")
    z, x = h // 4, lax.rem(h, 4)
    y, c = p // 2, lax.rem(p, 2)
    partner = p + 1 - 2 * c
    last = LAYERS - 1

    fac_in = pltpu.make_async_copy(factors, fac, lsem.at[0])
    cot_in = pltpu.make_async_copy(cot.at[pl.ds(pl.multiple_of(p * N, N), N)], gs.at[LAYERS], lsem.at[1])
    x_in = pltpu.make_async_copy(acts.at[pl.ds(pl.multiple_of(p * N, N), N)], xs.at[p], lsem.at[2])
    fac_in.start()
    cot_in.start()
    x_in.start()

    bar = pltpu.get_barrier_semaphore()

    def greet_hidden(k, _):
        pl.semaphore_signal(bar, inc=1, device_id={"hidden": lax.rem(h + k, PEERS)}, device_id_type=MESH)
        return 0

    def greet_pipe(k, _):
        pl.semaphore_signal(bar, inc=1, device_id={"pipe": lax.rem(p + k, LAYERS)}, device_id_type=MESH)
        return 0

    lax.fori_loop(1, PEERS, greet_hidden, 0)
    lax.fori_loop(1, LAYERS, greet_pipe, 0)

    fac_in.wait()

    def prepare(kind):
        if kind in (R1, R2):
            st[...] = fac[kind].astype(F32)
            for a in range(OWN):
                for cl in range(OWN):
                    rows = st[pl.ds(a * N + cl, N // OWN, stride=OWN), :]
                    wts[p, kind, pl.ds(a * N + cl * (N // OWN), N // OWN)] = rows.astype(BF)
        else:
            for b in range(OWN):
                wts[p, kind, blk(b)] = fac[kind, blk(b)].T

    for kind in (L2, R1, L1, R2):
        prepare(kind)
    pl.semaphore_wait(bar, PEERS - 1 + LAYERS - 1)

    def send_w(kind):
        def to(dest):
            pltpu.make_async_remote_copy(
                src_ref=wts.at[p, kind], dst_ref=wts.at[p, kind], send_sem=w_s.at[kind], recv_sem=w_r.at[p, kind],
                device_id={"pipe": dest}, device_id_type=MESH,
            ).start()

        to(lax.rem(p + 2, LAYERS))
        to(lax.rem(p + 6, LAYERS))
        if kind in RELAYED:
            pl.when(p < EARLY)(lambda: to(lax.rem(p + 4, LAYERS)))
        else:
            to(lax.rem(p + 4, LAYERS))
        to(partner)

    def send_x():
        def one(k, _):
            q = lax.rem(p + k, LAYERS)
            pltpu.make_async_remote_copy(
                src_ref=acts.at[pl.ds(pl.multiple_of(q * N, N), N)], dst_ref=xs.at[p], send_sem=x_s, recv_sem=x_r.at[p],
                device_id={"pipe": q}, device_id_type=MESH,
            ).start()
            return 0

        lax.fori_loop(1, LAYERS, one, 0)

    def fwd_copy(l, kind):
        return pltpu.make_async_remote_copy(
            src_ref=wts.at[l, kind], dst_ref=wts.at[l, kind], send_sem=f_s.at[l, kind], recv_sem=w_r.at[l, kind],
            device_id={"pipe": partner}, device_id_type=MESH,
        )

    def relay_copy(l, kind):
        return pltpu.make_async_remote_copy(
            src_ref=wts.at[l, kind], dst_ref=wts.at[l, kind], send_sem=y_s.at[l, kind], recv_sem=w_r.at[l, kind],
            device_id={"pipe": lax.rem(l + 4, LAYERS)}, device_id_type=MESH,
        )

    def relays(l):
        return jnp.logical_and(l >= EARLY, p == lax.rem(l + 6, LAYERS))

    def wait_w(l, kind):
        pltpu.make_async_copy(wts.at[l, kind], wts.at[l, kind], w_r.at[l, kind]).wait()

    def forward_w(l, kind):
        @pl.when(jnp.logical_and(lax.rem(l, 2) == c, l != p))
        def _():
            wait_w(l, kind)
            if kind in RELAYED:
                pl.when(relays(l))(lambda: relay_copy(l, kind).start())
            fwd_copy(l, kind).start()

    def need_w(l, kind):
        @pl.when(lax.rem(l, 2) != c)
        def _():
            wait_w(l, kind)

    def need_x(l):
        @pl.when(l == p)
        def _():
            x_in.wait()

        @pl.when(l != p)
        def _():
            pltpu.make_async_copy(xs.at[l], xs.at[l], x_r.at[l]).wait()

    def exchange(which, l):
        def one(k, _):
            i, j = k // 4, lax.rem(k, 4)
            hi, hj = (i + 1) // 2, (j + 1) // 2
            dz = 4 + hi * (1 - 2 * lax.rem(i, 2))
            dx = 2 + hj * (1 - 2 * lax.rem(j, 2))
            d = lax.rem(z + dz, 8) * 4 + lax.rem(x + dx, 4)
            pltpu.make_async_remote_copy(
                src_ref=send.at[which, l, pl.ds(pl.multiple_of(d * PIECE, PIECE), PIECE)],
                dst_ref=recv.at[which, l, pl.ds(pl.multiple_of(h * PIECE, PIECE), PIECE)],
                send_sem=a_s.at[which, l], recv_sem=a_r.at[which, l],
                device_id={"hidden": d}, device_id_type=MESH,
            ).start()
            return 0

        lax.fori_loop(0, PEERS - 1, one, 0, unroll=True)
        mine = pl.ds(pl.multiple_of(h * PIECE, PIECE), PIECE)
        recv[which, l, mine] = send[which, l, mine]

    def arrived(which, l):
        rows = recv.at[which, l, pl.ds(0, (PEERS - 1) * PIECE)]
        pltpu.make_async_copy(rows, rows, a_r.at[which, l]).wait()

    def produce_u(which, l, kind, value):
        for a in range(OWN):
            part = dot(wts[l, kind, blk(a)], value[:, a * N:(a + 1) * N], 1, 1)
            for cl in range(OWN):
                st[pl.ds(a * OWN + cl, PEERS, stride=PIECE), :] = part[cl * PEERS:(cl + 1) * PEERS]
        send[which, l] = st[...].astype(BF)

    def produce_d(which, l, kind, value):
        for b in range(OWN):
            st[pl.ds(b, N, stride=OWN), :] = dot(wts[l, kind, blk(b)], value[:, b * N:(b + 1) * N], 1, 1)
        send[which, l] = st[...].astype(BF)
        exchange(which, l)

    def take_u(which, l, out):
        arrived(which, l)
        st[...] = recv[which, l].astype(F32)
        for b in range(OWN):
            out[blk(b)] = st[pl.ds(b, N, stride=OWN), :].astype(BF)

    def take_d(which, l, out):
        arrived(which, l)
        st[...] = recv[which, l].astype(F32)
        for a in range(OWN):
            for cl in range(OWN):
                out[pl.ds(a * N + cl * PEERS, PEERS)] = st[pl.ds(a * OWN + cl, PEERS, stride=PIECE), :].astype(BF)

    def partial(l, kind, left, right):
        for b in range(OWN):
            pg[l, kind, blk(b)] = dot(left[blk(b)], right[:, blk(b)], 1, 0).astype(BF)

    def pair_copy(l, kind):
        return pltpu.make_async_remote_copy(
            src_ref=pg.at[l, kind, pl.ds(pl.multiple_of((1 - c) * HALF, HALF), HALF)], dst_ref=px.at[l, kind],
            send_sem=p_s.at[l, kind], recv_sem=p_r.at[l, kind], device_id={"pipe": partner}, device_id_type=MESH,
        )

    def home_copy(l, kind):
        return pltpu.make_async_remote_copy(
            src_ref=hs.at[l, kind], dst_ref=home.at[kind, p], send_sem=h_s.at[l, kind], recv_sem=h_r.at[kind],
            device_id={"pipe": l}, device_id_type=MESH,
        )

    def reduce(l, kind):
        pair_copy(l, kind).wait_recv()
        own = pg[l, kind, pl.ds(pl.multiple_of(c * HALF, HALF), HALF)]
        total = (own.astype(F32) + px[l, kind].astype(F32)).astype(BF)

        @pl.when(l == p)
        def _():
            home[kind, p] = total

        @pl.when(l != p)
        def _():
            hs[l, kind] = total
            home_copy(l, kind).start()

    def gin_copy(l):
        return pltpu.make_async_remote_copy(
            src_ref=gs.at[l], dst_ref=gin.at[pl.ds(pl.multiple_of(p * N, N), N)], send_sem=g_s.at[l], recv_sem=g_r,
            device_id={"pipe": l}, device_id_type=MESH,
        )

    def gin_own(l):
        return pltpu.make_async_copy(gs.at[l], gin.at[pl.ds(pl.multiple_of(p * N, N), N)], lsem.at[1])

    def first_half(l):
        need_w(l, R1)
        need_x(l)
        produce_u(U1, l, R1, xs[l])

    def second_half(l):
        slot = lax.rem(l, 2)
        need_w(l, L1)
        take_u(U1, l, vu1.at[slot])
        coeff = 0.7978845608028654
        for b in range(OWN):
            v = dot(vu1[slot, blk(b)], wts[l, L1, blk(b)], 0, 0)
            tangent = jnp.tanh(coeff * (v + 0.044715 * (v * v * v)))
            act[slot, :, b * N:(b + 1) * N] = (0.5 * v * (1.0 + tangent)).astype(BF)
            slope[:, b * N:(b + 1) * N] = 0.5 * (1.0 + tangent) + 0.5 * v * (1.0 - tangent * tangent) * coeff * (
                1.0 + 3.0 * 0.044715 * v * v
            )
        need_w(l, R2)
        produce_u(U2, l, R2, act[slot])

    def send_all():
        send_w(L2)
        send_w(R1)
        send_x()
        send_w(L1)
        send_w(R2)

    @pl.when(p == last)
    def _():
        send_all()

    cot_in.wait()
    forward_w(last, L2)

    def step(s, _):
        l = last - s
        slot = lax.rem(l, 2)
        need_w(l, L2)
        produce_d(D2, l, L2, gs[l + 1])

        @pl.when(jnp.logical_and(s >= 2, l >= 1))
        def _():
            exchange(U1, l - 1)

        @pl.when(s == 0)
        def _():
            pl.when(p == 5)(send_all)
            forward_w(l, R1)
            first_half(l)
            exchange(U1, l)
            pl.when(jnp.logical_or(p == 6, p < 5))(send_all)
            forward_w(l, L1)
            forward_w(l, R2)

        @pl.when(s <= 1)
        def _():
            second_half(l)

        @pl.when(s == 1)
        def _():
            forward_w(l - 1, R1)
            first_half(l - 1)
            exchange(U1, l - 1)

        @pl.when(s >= 1)
        def _():
            partial(l + 1, R1, vd1, xs.at[l + 1])
            pair_copy(l + 1, R1).start()
            take_u(U2, l + 1, vu2)
            partial(l + 1, L2, vu2, gs.at[l + 2])
            pair_copy(l + 1, L2).start()

            @pl.when(l >= 2)
            def _():
                forward_w(l - 2, R1)

            @pl.when(l >= 1)
            def _():
                forward_w(l - 1, L1)
                forward_w(l - 1, R2)
                forward_w(l - 1, L2)

        @pl.when(l == 0)
        def _():
            take_u(U2, l, vu2)
            partial(l, L2, vu2, gs.at[l + 1])
            pair_copy(l, L2).start()

        take_d(D2, l, vd2)
        for b in range(OWN):
            da = dot(vd2[blk(b)], wts[l, R2, blk(b)], 0, 0)
            dh[:, b * N:(b + 1) * N] = (da * slope[:, b * N:(b + 1) * N]).astype(BF)
        produce_d(D1, l, L1, dh[...])

        @pl.when(l >= 1)
        def _():
            exchange(U2, l)

        @pl.when(s == 0)
        def _():
            forward_w(l - 1, R1)
            first_half(l - 1)
            exchange(U1, l - 1)

        partial(l, R2, vd2, act.at[slot])
        pair_copy(l, R2).start()
        partial(l, L1, vu1.at[slot], dh)
        pair_copy(l, L1).start()

        @pl.when(jnp.logical_and(s >= 1, l >= 1))
        def _():
            second_half(l - 1)

        @pl.when(jnp.logical_and(s >= 1, l >= 2))
        def _():
            first_half(l - 2)

        @pl.when(l == 1)
        def _():
            exchange(U2, l - 1)

        @pl.when(s == 0)
        def _():
            forward_w(l - 1, L1)
            forward_w(l - 1, R2)
            forward_w(l - 1, L2)

        @pl.when(s >= 1)
        def _():
            reduce(l + 1, R1)
            reduce(l + 1, L2)

        pl.when(l == 0)(lambda: reduce(l, L2))

        reduce(l, R2)
        reduce(l, L1)

        take_d(D1, l, vd1)

        @pl.when(l == 0)
        def _():
            partial(l, R1, vd1, xs.at[l])
            pair_copy(l, R1).start()

        for b in range(OWN):
            dx = dot(vd1[blk(b)], wts[l, R1, blk(b)], 0, 0)
            gs[l, :, b * N:(b + 1) * N] = (gs[l + 1, :, b * N:(b + 1) * N].astype(F32) + dx).astype(BF)

        @pl.when(l == p)
        def _():
            gin_own(l).start()

        @pl.when(l != p)
        def _():
            gin_copy(l).start()

        return 0

    lax.fori_loop(0, LAYERS, step, 0)

    reduce(0, R1)

    def finish(kind):
        seven = home.at[kind, pl.ds(0, LAYERS - 1)]
        pltpu.make_async_copy(seven, seven, h_r.at[kind]).wait()
        for half in range(2):
            total = home[kind, half].astype(F32)
            for group in range(1, LAYERS // 2):
                total = total + home[kind, 2 * group + half].astype(F32)
            total = total * (LAYERS * N) ** -0.5
            for b in range(2):
                i = half * 2 + b
                own = total[b * N:(b + 1) * N]
                if kind in (R1, R2):
                    for cl in range(OWN):
                        fin[kind, pl.ds(i * N + cl, PEERS, stride=OWN), :] = own[cl * PEERS:(cl + 1) * PEERS]
                else:
                    fin[kind, blk(i)] = own.T
        out = pltpu.make_async_copy(fin.at[kind], gfac.at[kind], lsem.at[3 + kind])
        out.start()
        return out

    outs = [finish(kind) for kind in (R2, L1, L2, R1)]
    for out in outs:
        out.wait()

    seven = gin.at[pl.ds(0, (LAYERS - 1) * N)]
    pltpu.make_async_copy(seven, seven, g_r).wait()
    gin_own(p).wait()

    def drain(l, _):
        for which in range(4):
            rows = send.at[which, l, pl.ds(0, (PEERS - 1) * PIECE)]
            pltpu.make_async_copy(rows, rows, a_s.at[which, l]).wait()
        for kind in range(4):
            pair_copy(l, kind).wait_send()

            @pl.when(l != p)
            def _():
                home_copy(l, kind).wait_send()

            @pl.when(jnp.logical_and(lax.rem(l, 2) == c, l != p))
            def _():
                fwd_copy(l, kind).wait_send()
                if kind in RELAYED:
                    pl.when(relays(l))(lambda: relay_copy(l, kind).wait_send())

        @pl.when(l != p)
        def _():
            gin_copy(l).wait_send()

        return 0

    lax.fori_loop(0, LAYERS, drain, 0)
    def sent(kind, copies):
        part = wts.at[p, pl.ds(0, copies)]
        pltpu.make_async_copy(part, part, w_s.at[kind]).wait()

    for kind in range(4):
        if kind in RELAYED:
            pl.when(p < EARLY)(lambda: sent(kind, 4))
            pl.when(p >= EARLY)(lambda: sent(kind, 3))
        else:
            sent(kind, 4)
    pltpu.make_async_copy(seven, seven, x_s).wait()


def shards(acts, factors, cotangent):
    dma = pltpu.SemaphoreType.DMA
    gin, gfac = pl.pallas_call(
        kernel,
        name="monarch_backward",
        out_shape=(
            jax.ShapeDtypeStruct((LAYERS * N, FEAT), BF),
            jax.ShapeDtypeStruct((4, FEAT, N), F32),
        ),
        in_specs=[pl.BlockSpec(memory_space=pl.ANY)] * 3,
        out_specs=(pl.BlockSpec(memory_space=pl.ANY), pl.BlockSpec(memory_space=pl.ANY)),
        scratch_shapes=[
            pltpu.VMEM((4, FEAT, N), BF),
            pltpu.VMEM((LAYERS, 4, FEAT, N), BF),
            pltpu.VMEM((LAYERS, N, FEAT), BF),
            pltpu.VMEM((LAYERS + 1, N, FEAT), BF),
            pltpu.VMEM((4, LAYERS, FEAT, N), BF),
            pltpu.VMEM((4, LAYERS, FEAT, N), BF),
            pltpu.VMEM((FEAT, N), F32),
            pltpu.VMEM((2, FEAT, N), BF),
            pltpu.VMEM((FEAT, N), BF),
            pltpu.VMEM((FEAT, N), BF),
            pltpu.VMEM((FEAT, N), BF),
            pltpu.VMEM((2, N, FEAT), BF),
            pltpu.VMEM((N, FEAT), F32),
            pltpu.VMEM((N, FEAT), BF),
            pltpu.VMEM((LAYERS, 4, FEAT, N), BF),
            pltpu.VMEM((LAYERS, 4, HALF, N), BF),
            pltpu.VMEM((LAYERS, 4, HALF, N), BF),
            pltpu.VMEM((4, LAYERS, HALF, N), BF),
            pltpu.VMEM((4, FEAT, N), F32),
            dma((7,)),
            dma((4, LAYERS)), dma((4, LAYERS)),
            dma((4,)), dma((LAYERS, 4)), dma((LAYERS, 4)), dma((LAYERS, 4)),
            dma, dma((LAYERS,)),
            dma((LAYERS,)), dma,
            dma((LAYERS, 4)), dma((LAYERS, 4)),
            dma((LAYERS, 4)), dma((4,)),
        ],
        compiler_params=pltpu.CompilerParams(
            collective_id=0, has_side_effects=True, vmem_limit_bytes=63 * 2**20
        ),
    )(acts.reshape(LAYERS * N, FEAT), factors.reshape(4, FEAT, N), cotangent)
    return gin.reshape(1, LAYERS * N, FEAT), gfac.reshape(1, 4, OWN, N, N)


def solution(mesh):
    in_specs = (P("pipe", None, "hidden"), P("pipe", None, "hidden", None, None), P(None, "hidden"))
    out_specs = (P("pipe", None, "hidden"), P("pipe", None, "hidden", None, None))
    return jax.shard_map(shards, mesh=mesh, in_specs=in_specs, out_specs=out_specs, check_vma=False)
```
